32 devices in a mesh: seq: 8 (over z, y), chan: 4 (over x, core).
Axes of the slice: x: 2, y: 2, z: 4, core: 2. Of those that a mesh axis runs over, the one named last changes fastest.
Arguments:
- output_gate: bfloat16 [256, 16384], P('chan', 'seq'), may hold values from -6 to 6
- input_gate: bfloat16 [256, 16384], P('chan', 'seq'), may hold values from -6 to 6
- signal: bfloat16 [256, 16384], P('chan', 'seq'), may hold values from -6 to 6
- cotangent: bfloat16 [256, 16384], P('chan', 'seq'), may hold values from -6 to 6
- long_filter: float32 [64, 16384], P(None, 'seq'), may hold values from -1 to 1
Outputs:
- grad_output_gate: bfloat16 [256, 16384], P('chan', 'seq')
- grad_input_gate: bfloat16 [256, 16384], P('chan', 'seq')
- grad_signal: bfloat16 [256, 16384], P('chan', 'seq')
- grad_filter: float32 [64, 16384], P('chan', 'seq')
The draws below stay inside these ranges and needn't reach their ends.
All inputs are finite; a program needn't handle non-finite values.
Results may differ from the reference program's by a relative error of at most 0.0022.
Values sent between devices are 32-bit elements; how exact they have to be, the bound alone decides.
A program may use at most 128 MiB of HBM per device.

```python
import math
import jax
import jax.numpy as jnp

CHANNELS = 256
FILTERS = 64
TOKENS = 16384


def draw_long_filter(key, part):
    key = jax.random.fold_in(key, 7)
    rate_key, noise_key = jax.random.split(key)
    slow_key = jax.random.fold_in(key, 11)
    weight_key = jax.random.fold_in(key, 13)
    places = jnp.arange(TOKENS, dtype=jnp.float32)[None, :]
    log_rate = jax.random.uniform(rate_key, (FILTERS, 1), jnp.float32, math.log(1.0 / TOKENS), math.log(1.0 / 32.0))
    noise = jax.random.truncated_normal(noise_key, -3.5, 3.5, (FILTERS, TOKENS), jnp.float32)
    decay = jnp.exp(log_rate)
    slow_log = jax.random.uniform(slow_key, (FILTERS, 1), jnp.float32, math.log(0.5 / TOKENS), math.log(2.0 / TOKENS))
    slow_rate = jnp.exp(slow_log)
    slow_weight = jax.random.uniform(weight_key, (FILTERS, 1), jnp.float32, 0.2, 0.4)
    envelope = jnp.sqrt(2.0 * decay) * jnp.exp(-decay * places) + slow_weight * jnp.sqrt(2.0 * slow_rate) * jnp.exp(-slow_rate * places)
    return noise * envelope


def block_scale(key, shape, cuts, least, largest):
    gain = 1.0
    for position, parts in cuts:
        steps = jax.random.uniform(jax.random.fold_in(jax.random.fold_in(key, 6), position), (parts,), jnp.float32, least / len(cuts), largest / len(cuts))
        gain = gain * jnp.repeat(jnp.exp(steps), shape[position] // parts).reshape((-1,) + (1,) * (len(shape) - 1 - position))
    return gain


def gaussian(stream_key, shape, deviation, most, shards=(), held_as=jnp.bfloat16):
    factor_of = block_scale(stream_key, shape, shards, -0.22, 0.18) if shards else 1.0
    drawn = jax.random.normal(stream_key, shape, jnp.float32) * deviation * factor_of
    return jnp.minimum(jnp.maximum(drawn, -most), most).astype(held_as)


def setup_inputs(seed: int = 0) -> dict:
    key_of = jax.random.split(jax.random.key(seed), 6)
    output_gate = gaussian(key_of[0], (CHANNELS, TOKENS), 1.0, 6.0, ((0, 4), (1, 8)))
    input_gate = gaussian(key_of[1], (CHANNELS, TOKENS), 1.0, 6.0, ((0, 4), (1, 8)))
    signal = gaussian(key_of[2], (CHANNELS, TOKENS), 1.0, 6.0, ((0, 4), (1, 8)))
    cotangent = gaussian(key_of[3], (CHANNELS, TOKENS), 1.0, 6.0, ((0, 4), (1, 8)))
    long_filter = draw_long_filter(jax.random.fold_in(key_of[5], 71), 0)
    return dict(output_gate=output_gate, input_gate=input_gate, signal=signal, cotangent=cotangent, long_filter=long_filter)


def reference(output_gate, input_gate, signal, cotangent, long_filter):
    length = 2 * TOKENS
    mixed = input_gate.astype(jnp.float32) * signal.astype(jnp.float32)
    gated = cotangent.astype(jnp.float32) * output_gate.astype(jnp.float32)
    spread = jnp.tile(long_filter, (CHANNELS // FILTERS, 1))
    mixed_spec = jnp.fft.rfft(mixed, n=length, axis=-1)
    gated_spec = jnp.fft.rfft(gated, n=length, axis=-1)
    filter_spec = jnp.fft.rfft(spread, n=length, axis=-1)
    response = jnp.fft.irfft(filter_spec * mixed_spec, n=length, axis=-1)[:, :TOKENS].astype(jnp.float32)
    grad_mixed = jnp.fft.irfft(jnp.conj(filter_spec) * gated_spec, n=length, axis=-1)[:, :TOKENS].astype(jnp.float32)
    kernel = jnp.fft.irfft(jnp.conj(mixed_spec) * gated_spec, n=length, axis=-1)[:, :TOKENS].astype(jnp.float32)
    grad_filter = kernel.reshape(CHANNELS // FILTERS, FILTERS, TOKENS).sum(axis=0) / math.sqrt(TOKENS)
    grad_output_gate = (cotangent.astype(jnp.float32) * response).astype(jnp.bfloat16)
    grad_input_gate = (grad_mixed * signal.astype(jnp.float32)).astype(jnp.bfloat16)
    grad_signal = (grad_mixed * input_gate.astype(jnp.float32)).astype(jnp.bfloat16)
    return (grad_output_gate, grad_input_gate, grad_signal, grad_filter.astype(jnp.float32))
```

```python
import functools
import math

import jax
import jax.numpy as jnp
import numpy as np
from jax import lax
from jax.experimental import pallas as pl
from jax.experimental.pallas import tpu as pltpu
from jax.sharding import PartitionSpec as P


def split_bf16(value):
    high = value.astype(jnp.bfloat16)
    return high, (value - high.astype(jnp.float32)).astype(jnp.bfloat16)


def tables(rows, cols):
    total = rows * cols
    row = np.arange(rows)
    col = np.arange(cols)
    angle = 2.0 * np.pi * ((4 * row[:, None] + 1) * row[None, :] % (4 * rows)) / (4 * rows)
    first = np.concatenate([np.cos(angle), -np.sin(angle)], axis=0)
    angle = 2.0 * np.pi * (col[:, None] * col[None, :] % cols) / cols
    cos, sin = np.cos(angle), np.sin(angle)
    second = np.block([[cos, -sin], [sin, cos]])
    angle = 2.0 * np.pi * ((4 * row[:, None] + 1) * col[None, :]) / (4 * total)
    twist = np.stack([np.cos(angle), -np.sin(angle)]).astype(np.float32)
    out = []
    for table in (first, second, second.T, first.T / total):
        out += list(split_bf16(jnp.asarray(table.astype(np.float32))))
    return out + [jnp.asarray(twist)]


def product(left, right):
    dot = functools.partial(jnp.dot, preferred_element_type=jnp.float32)
    return dot(left[0], right[0]) + dot(left[0], right[1]) + dot(left[1], right[0])


def transform_kernel(
    repeat, rows, cols, kernel_scale,
    mixed_ref, gated_ref, filter_ref,
    first_hi, first_lo, second_hi, second_lo, back_hi, back_lo, last_hi, last_lo, twist_ref,
    response_ref, grad_ref, kernel_ref,
):
    first = (first_hi[...], first_lo[...])
    second = (second_hi[...], second_lo[...])
    back = (back_hi[...], back_lo[...])
    last = (last_hi[...], last_lo[...])
    twist_re = twist_ref[0]
    twist_im = twist_ref[1]

    def forward(block):
        part = product(first, split_bf16(block))
        re, im = part[:rows], part[rows:]
        turned = jnp.concatenate(
            [re * twist_re - im * twist_im, re * twist_im + im * twist_re], axis=1
        )
        spec = product(split_bf16(turned), second)
        return spec[:, :cols], spec[:, cols:]

    def inverse(re, im):
        part = product(split_bf16(jnp.concatenate([re, im], axis=1)), back)
        re, im = part[:, :cols], part[:, cols:]
        turned = jnp.concatenate(
            [re * twist_re + im * twist_im, im * twist_re - re * twist_im], axis=0
        )
        return product(last, split_bf16(turned))

    h_re, h_im = forward(filter_ref[0])
    k_re = k_im = 0.0
    for place in range(repeat):
        m_re, m_im = forward(mixed_ref[0, place])
        g_re, g_im = forward(gated_ref[0, place])
        response_ref[0, place] = inverse(h_re * m_re - h_im * m_im, h_re * m_im + h_im * m_re)
        grad_ref[0, place] = inverse(h_re * g_re + h_im * g_im, h_re * g_im - h_im * g_re)
        k_re += m_re * g_re + m_im * g_im
        k_im += m_re * g_im - m_im * g_re
    kernel_ref[0] = inverse(k_re, k_im) * kernel_scale


def transform(mixed, gated, filters):
    count, repeat, rows, cols = mixed.shape
    constants = tables(rows, cols)
    whole = [
        pl.BlockSpec(table.shape, lambda i, rank=table.ndim: (0,) * rank) for table in constants
    ]
    many = pl.BlockSpec((1, repeat, rows, cols), lambda i: (i, 0, 0, 0))
    one = pl.BlockSpec((1, rows, cols), lambda i: (i, 0, 0))
    total = rows * cols
    return pl.pallas_call(
        functools.partial(transform_kernel, repeat, rows, cols, 1.0 / math.sqrt(total)),
        grid=(count,),
        in_specs=[many, many, one] + whole,
        out_specs=[many, many, one],
        out_shape=[
            jax.ShapeDtypeStruct(mixed.shape, jnp.float32),
            jax.ShapeDtypeStruct(mixed.shape, jnp.float32),
            jax.ShapeDtypeStruct(filters.shape, jnp.float32),
        ],
        compiler_params=pltpu.CompilerParams(vmem_limit_bytes=48 * 1024 * 1024),
        name="transform",
    )(mixed, gated, filters, *constants)


def per_device(output_gate, input_gate, signal, cotangent, long_filter):
    seq_count = lax.axis_size("seq")
    chan_count = lax.axis_size("chan")
    channels, tok_local = signal.shape
    filters = long_filter.shape[0]
    tokens = tok_local * seq_count
    cols = 2 ** (int(math.log2(tokens)) // 2)
    rows = tokens // cols
    rows_dev = rows // seq_count
    spread = channels == filters and filters % (seq_count * chan_count) == 0
    repeat = chan_count if spread else 1
    axes = ("chan", "seq") if spread else ("seq",)
    parts = seq_count * repeat
    held = filters // parts

    mixed = input_gate.astype(jnp.float32) * signal.astype(jnp.float32)
    gated = cotangent.astype(jnp.float32) * output_gate.astype(jnp.float32)
    stacked = jnp.stack([mixed, gated], axis=0).reshape(2, parts, held, rows_dev, cols)
    pieces = lax.all_to_all(stacked.transpose(1, 0, 2, 3, 4), axes, 0, 0)
    pieces = pieces.reshape(repeat, seq_count, 2, held, rows_dev, cols)
    pieces = pieces.transpose(2, 3, 0, 1, 4, 5).reshape(2, held, repeat, rows, cols)
    if spread:
        span = held * seq_count
        long_filter = lax.dynamic_slice_in_dim(
            long_filter, lax.axis_index("chan") * span, span, axis=0
        )
    taps = long_filter.reshape(seq_count, held, rows_dev, cols)
    taps = lax.all_to_all(taps, "seq", 0, 0).transpose(1, 0, 2, 3).reshape(held, rows, cols)

    response, grad_mixed, kernel = transform(pieces[0], pieces[1], taps)

    kernel = kernel.reshape(held, seq_count, rows_dev, cols).transpose(1, 0, 2, 3)
    kernel = lax.all_to_all(kernel, "seq", 0, 0).reshape(held * seq_count, tok_local)
    if not spread:
        kernel = lax.psum_scatter(kernel, "chan", scatter_dimension=0, tiled=True)
    results = jnp.stack([response, grad_mixed]).reshape(
        2, held, repeat, seq_count, rows_dev, cols
    )
    results = results.transpose(2, 3, 0, 1, 4, 5).reshape(parts, 2, held, rows_dev, cols)
    results = lax.all_to_all(results, axes, 0, 0)
    results = results.transpose(1, 0, 2, 3, 4).reshape(2, channels, tok_local)
    response, grad_mixed = results[0], results[1]
    grad_output_gate = (cotangent.astype(jnp.float32) * response).astype(jnp.bfloat16)
    grad_input_gate = (grad_mixed * signal.astype(jnp.float32)).astype(jnp.bfloat16)
    grad_signal = (grad_mixed * input_gate.astype(jnp.float32)).astype(jnp.bfloat16)
    return (grad_output_gate, grad_input_gate, grad_signal, kernel)


def solution(mesh):
    placed = (
        P("chan", "seq"),
        P("chan", "seq"),
        P("chan", "seq"),
        P("chan", "seq"),
        P(None, "seq"),
    )
    return jax.shard_map(
        per_device,
        mesh=mesh,
        in_specs=placed,
        out_specs=(P("chan", "seq"), P("chan", "seq"), P("chan", "seq"), P("chan", "seq")),
        check_vma=False,
    )
```

```python
import functools
import math

import jax
import jax.numpy as jnp
import numpy as np
from jax import lax
from jax.experimental import pallas as pl
from jax.experimental.pallas import tpu as pltpu
from jax.sharding import PartitionSpec as P


def split_bf16(value):
    high = value.astype(jnp.bfloat16)
    return high, (value - high.astype(jnp.float32)).astype(jnp.bfloat16)


def tables(rows, cols):
    total = rows * cols
    row = np.arange(rows)
    col = np.arange(cols)
    angle = 2.0 * np.pi * ((4 * row[:, None] + 1) * row[None, :] % (4 * rows)) / (4 * rows)
    first = np.concatenate([np.cos(angle), -np.sin(angle)], axis=0)
    angle = 2.0 * np.pi * (col[:, None] * col[None, :] % cols) / cols
    cos, sin = np.cos(angle), np.sin(angle)
    second = np.block([[cos, -sin], [sin, cos]])
    angle = 2.0 * np.pi * ((4 * row[:, None] + 1) * col[None, :]) / (4 * total)
    twist = np.stack([np.cos(angle), -np.sin(angle)]).astype(np.float32)
    out = []
    for table in (first, second, second.T, first.T / total):
        out += list(split_bf16(jnp.asarray(table.astype(np.float32))))
    return out + [jnp.asarray(twist)]


def product(left, right):
    dot = functools.partial(jnp.dot, preferred_element_type=jnp.float32)
    return dot(left[0], right[0]) + dot(left[0], right[1]) + dot(left[1], right[0])


def transform_channels(tables_in, mixed, gated, taps, scale):
    first, second, back, last, twist_re, twist_im = tables_in
    rows, cols = twist_re.shape

    def forward(block):
        part = product(first, split_bf16(block))
        re, im = part[:rows], part[rows:]
        turned = jnp.concatenate(
            [re * twist_re - im * twist_im, re * twist_im + im * twist_re], axis=1
        )
        spec = product(split_bf16(turned), second)
        return spec[:, :cols], spec[:, cols:]

    def inverse(re, im):
        part = product(split_bf16(jnp.concatenate([re, im], axis=1)), back)
        re, im = part[:, :cols], part[:, cols:]
        turned = jnp.concatenate(
            [re * twist_re + im * twist_im, im * twist_re - re * twist_im], axis=0
        )
        return product(last, split_bf16(turned))

    h_re, h_im = forward(taps())
    k_re = k_im = 0.0
    pairs = []
    for mixed_one, gated_one in zip(mixed, gated):
        m_re, m_im = forward(mixed_one())
        g_re, g_im = forward(gated_one())
        response = inverse(h_re * m_re - h_im * m_im, h_re * m_im + h_im * m_re)
        grad = inverse(h_re * g_re + h_im * g_im, h_re * g_im - h_im * g_re)
        k_re += m_re * g_re + m_im * g_im
        k_im += m_re * g_im - m_im * g_re
        pairs.append((response, grad))
    return pairs, inverse(k_re, k_im) * scale


def exchange_kernel(
    repeat, seq_count, held, scale,
    send_ref, taps_ref,
    first_hi, first_lo, second_hi, second_lo, back_hi, back_lo, last_hi, last_lo, twist_ref,
    result_ref, kernel_ref,
    seqs, taps_all, outs, kernels,
    in_sem, taps_sem, out_sem, kernel_sem, in_sent, taps_sent, out_sent, kernel_sent,
):
    parts = repeat * seq_count
    rows_dev = taps_ref.shape[-2]
    seq_me = lax.axis_index("seq")
    chan_me = lax.axis_index("chan")
    place_me = seq_me + (chan_me * seq_count if repeat > 1 else 0)
    source_me = chan_me if repeat > 1 else 0

    def device(part):
        chan = part // seq_count if repeat > 1 else chan_me
        return {"seq": part % seq_count, "chan": chan}

    def chan_of(part):
        return part // seq_count if repeat > 1 else 0

    def span(seq):
        return pl.ds(pl.multiple_of(seq * rows_dev, rows_dev), rows_dev)

    def peer(step):
        return lax.rem(place_me + step, parts)

    def seq_peer(step):
        return lax.rem(seq_me + step, seq_count)

    barrier = pltpu.get_barrier_semaphore()

    @pl.loop(1, parts)
    def _(step):
        pl.semaphore_signal(
            barrier, inc=1, device_id=device(peer(step)), device_id_type=pl.DeviceIdType.MESH
        )

    pl.semaphore_wait(barrier, parts - 1)

    def send_in(index):
        pltpu.make_async_copy(
            taps_ref.at[seq_me, index], taps_all.at[index, span(seq_me)], taps_sem.at[index]
        ).start()

        @pl.loop(1, seq_count)
        def _(step):
            to = seq_peer(step)
            pltpu.make_async_remote_copy(
                src_ref=taps_ref.at[to, index],
                dst_ref=taps_all.at[index, span(seq_me)],
                send_sem=taps_sent.at[index],
                recv_sem=taps_sem.at[index],
                device_id={"seq": to, "chan": chan_me},
                device_id_type=pl.DeviceIdType.MESH,
            ).start()

        pltpu.make_async_copy(
            send_ref.at[place_me, index],
            seqs.at[index, :, source_me, span(seq_me)],
            in_sem.at[index],
        ).start()

        @pl.loop(1, parts)
        def _(step):
            to = peer(step)
            pltpu.make_async_remote_copy(
                src_ref=send_ref.at[to, index],
                dst_ref=seqs.at[index, :, source_me, span(seq_me)],
                send_sem=in_sent.at[index],
                recv_sem=in_sem.at[index],
                device_id=device(to),
                device_id_type=pl.DeviceIdType.MESH,
            ).start()

    def send_out(index):
        mine = place_me * held + index
        pltpu.make_async_copy(
            kernels.at[index, span(seq_me)],
            kernel_ref.at[seq_me * held + index],
            kernel_sem,
        ).start()

        @pl.loop(1, seq_count)
        def _(step):
            to = seq_peer(step)
            pltpu.make_async_remote_copy(
                src_ref=kernels.at[index, span(to)],
                dst_ref=kernel_ref.at[seq_me * held + index],
                send_sem=kernel_sent.at[index],
                recv_sem=kernel_sem,
                device_id={"seq": to, "chan": chan_me},
                device_id_type=pl.DeviceIdType.MESH,
            ).start()

        pltpu.make_async_copy(
            outs.at[index, :, source_me, span(seq_me)], result_ref.at[:, mine], out_sem
        ).start()

        @pl.loop(1, parts)
        def _(step):
            to = peer(step)
            pltpu.make_async_remote_copy(
                src_ref=outs.at[index, :, chan_of(to), span(to % seq_count)],
                dst_ref=result_ref.at[:, mine],
                send_sem=out_sent.at[index],
                recv_sem=out_sem,
                device_id=device(to),
                device_id_type=pl.DeviceIdType.MESH,
            ).start()

    def finish(ref, sem):
        pltpu.make_async_copy(ref, ref, sem).wait()

    for index in range(held):
        send_in(index)

    tables_in = (
        (first_hi[...], first_lo[...]),
        (second_hi[...], second_lo[...]),
        (back_hi[...], back_lo[...]),
        (last_hi[...], last_lo[...]),
        twist_ref[0],
        twist_ref[1],
    )

    for index in range(held):
        finish(taps_all.at[index], taps_sem.at[index])
        finish(seqs.at[index], in_sem.at[index])
        mixed = [functools.partial(lambda c: seqs[index, 0, c], c) for c in range(repeat)]
        gated = [functools.partial(lambda c: seqs[index, 1, c], c) for c in range(repeat)]
        pairs, kernel = transform_channels(
            tables_in, mixed, gated, lambda: taps_all[index], scale
        )
        for chan, (response, grad) in enumerate(pairs):
            outs[index, 0, chan] = response
            outs[index, 1, chan] = grad
        kernels[index] = kernel
        send_out(index)

    for index in range(held):
        finish(send_ref.at[pl.ds(0, parts - 1), index], in_sent.at[index])
        finish(taps_ref.at[pl.ds(0, seq_count - 1), index], taps_sent.at[index])
        finish(send_ref.at[pl.ds(0, parts - 1), index], out_sent.at[index])
        finish(taps_ref.at[pl.ds(0, seq_count - 1), index], kernel_sent.at[index])
    finish(kernel_ref, kernel_sem)
    finish(result_ref, out_sem)


def exchange(send, taps, repeat, rows, cols):
    parts, held, _, rows_dev, _ = send.shape
    seq_count = parts // repeat
    constants = tables(rows, cols)
    vmem = pl.BlockSpec(memory_space=pltpu.VMEM)
    hbm = pl.BlockSpec(memory_space=pl.ANY)
    f32 = jnp.float32
    dma = pltpu.SemaphoreType.DMA
    moved = 2 * 4 * (send.size + taps.size)
    return pl.pallas_call(
        functools.partial(
            exchange_kernel, repeat, seq_count, held, 1.0 / math.sqrt(rows * cols)
        ),
        in_specs=[vmem] * (2 + len(constants)),
        out_specs=[hbm, hbm],
        out_shape=[
            jax.ShapeDtypeStruct((2, parts * held, rows_dev, cols), f32),
            jax.ShapeDtypeStruct((seq_count * held, rows_dev, cols), f32),
        ],
        scratch_shapes=[
            pltpu.VMEM((held, 2, repeat, rows, cols), f32),
            pltpu.VMEM((held, rows, cols), f32),
            pltpu.VMEM((held, 2, repeat, rows, cols), f32),
            pltpu.VMEM((held, rows, cols), f32),
            dma((held,)), dma((held,)), dma(()), dma(()),
            dma((held,)), dma((held,)), dma((held,)), dma((held,)),
        ],
        compiler_params=pltpu.CompilerParams(
            collective_id=0, has_side_effects=True, vmem_limit_bytes=48 * 1024 * 1024
        ),
        cost_estimate=pl.CostEstimate(
            flops=12 * send.size * (rows + cols) * 4, bytes_accessed=moved, transcendentals=0
        ),
        name="exchange",
    )(send, taps, *constants)


def per_device(output_gate, input_gate, signal, cotangent, long_filter):
    seq_count = lax.axis_size("seq")
    chan_count = lax.axis_size("chan")
    channels, tok_local = signal.shape
    filters = long_filter.shape[0]
    tokens = tok_local * seq_count
    cols = 2 ** (int(math.log2(tokens)) // 2)
    rows = tokens // cols
    rows_dev = rows // seq_count
    spread = channels == filters and filters % (seq_count * chan_count) == 0
    repeat = chan_count if spread else 1
    parts = seq_count * repeat
    held = filters // parts

    mixed = input_gate.astype(jnp.float32) * signal.astype(jnp.float32)
    gated = cotangent.astype(jnp.float32) * output_gate.astype(jnp.float32)
    send = jnp.stack([mixed, gated], axis=0).reshape(2, parts, held, rows_dev, cols)
    send = send.transpose(1, 2, 0, 3, 4)
    if spread:
        block = held * seq_count
        long_filter = lax.dynamic_slice_in_dim(
            long_filter, lax.axis_index("chan") * block, block, axis=0
        )
    taps = long_filter.reshape(seq_count, held, rows_dev, cols)

    results, kernel = exchange(send, taps, repeat, rows, cols)

    kernel = kernel.reshape(held * seq_count, tok_local)
    if not spread:
        kernel = lax.psum_scatter(kernel, "chan", scatter_dimension=0, tiled=True)
    response, grad_mixed = results.reshape(2, channels, tok_local)
    grad_output_gate = (cotangent.astype(jnp.float32) * response).astype(jnp.bfloat16)
    grad_input_gate = (grad_mixed * signal.astype(jnp.float32)).astype(jnp.bfloat16)
    grad_signal = (grad_mixed * input_gate.astype(jnp.float32)).astype(jnp.bfloat16)
    return (grad_output_gate, grad_input_gate, grad_signal, kernel)


def solution(mesh):
    placed = (
        P("chan", "seq"),
        P("chan", "seq"),
        P("chan", "seq"),
        P("chan", "seq"),
        P(None, "seq"),
    )
    return jax.shard_map(
        per_device,
        mesh=mesh,
        in_specs=placed,
        out_specs=(P("chan", "seq"), P("chan", "seq"), P("chan", "seq"), P("chan", "seq")),
        check_vma=False,
    )
```

```python
import functools
import math

import jax
import jax.numpy as jnp
import numpy as np
from jax import lax
from jax.experimental import pallas as pl
from jax.experimental.pallas import tpu as pltpu
from jax.sharding import PartitionSpec as P


def split_bf16(value):
    high = value.astype(jnp.bfloat16)
    return high, (value - high.astype(jnp.float32)).astype(jnp.bfloat16)


def tables(rows, cols):
    total = rows * cols
    row = np.arange(rows)
    col = np.arange(cols)
    angle = 2.0 * np.pi * ((4 * row[:, None] + 1) * row[None, :] % (4 * rows)) / (4 * rows)
    first = np.concatenate([np.cos(angle), -np.sin(angle)], axis=0)
    angle = 2.0 * np.pi * (col[:, None] * col[None, :] % cols) / cols
    cos, sin = np.cos(angle), np.sin(angle)
    second = np.block([[cos, -sin], [sin, cos]])
    angle = 2.0 * np.pi * ((4 * row[:, None] + 1) * col[None, :]) / (4 * total)
    twist = np.stack([np.cos(angle), -np.sin(angle)]).astype(np.float32)
    out = []
    for table in (first, second, second.T, first.T / total):
        out += list(split_bf16(jnp.asarray(table.astype(np.float32))))
    return out + [jnp.asarray(twist)]


def product(left, right):
    dot = functools.partial(jnp.dot, preferred_element_type=jnp.float32)
    return dot(left[0], right[0]) + dot(left[0], right[1]) + dot(left[1], right[0])


def transform_channels(tables_in, mixed, gated, taps, scale):
    first, second, back, last, twist_re, twist_im = tables_in
    rows, cols = twist_re.shape

    def forward(block):
        part = product(first, split_bf16(block))
        re, im = part[:rows], part[rows:]
        turned = jnp.concatenate(
            [re * twist_re - im * twist_im, re * twist_im + im * twist_re], axis=1
        )
        spec = product(split_bf16(turned), second)
        return spec[:, :cols], spec[:, cols:]

    def inverse(re, im):
        part = product(split_bf16(jnp.concatenate([re, im], axis=1)), back)
        re, im = part[:, :cols], part[:, cols:]
        turned = jnp.concatenate(
            [re * twist_re + im * twist_im, im * twist_re - re * twist_im], axis=0
        )
        return product(last, split_bf16(turned))

    h_re, h_im = forward(taps())
    k_re = k_im = 0.0
    pairs = []
    for mixed_one, gated_one in zip(mixed, gated):
        m_re, m_im = forward(mixed_one())
        g_re, g_im = forward(gated_one())
        response = inverse(h_re * m_re - h_im * m_im, h_re * m_im + h_im * m_re)
        grad = inverse(h_re * g_re + h_im * g_im, h_re * g_im - h_im * g_re)
        k_re += m_re * g_re + m_im * g_im
        k_im += m_re * g_im - m_im * g_re
        pairs.append((response, grad))
    return pairs, inverse(k_re, k_im) * scale


def exchange_kernel(
    repeat, seq_count, held, rows_dev, scale,
    output_gate_ref, input_gate_ref, signal_ref, cotangent_ref, filter_ref, *refs,
):
    constants = refs[:9]
    result_ref, kernel_ref = refs[9:11]
    tables_ref = refs[11:20]
    (
        output_gate, input_gate, signal, cotangent, filter_rows, send_ref, taps_ref,
        seqs, taps_all, outs, kernels,
        load_sem, table_sem, in_sem, taps_sem, out_sem, kernel_sem,
        in_sent, taps_sent, out_sent, kernel_sent,
    ) = refs[20:]
    parts = repeat * seq_count
    wide = 2 * rows_dev
    channels = signal.shape[0]
    seq_me = lax.axis_index("seq")
    chan_me = lax.axis_index("chan")
    place_me = seq_me + (chan_me * seq_count if repeat > 1 else 0)
    source_me = chan_me if repeat > 1 else 0

    def device(part):
        chan = part // seq_count if repeat > 1 else chan_me
        return {"seq": part % seq_count, "chan": chan}

    def chan_of(part):
        return part // seq_count if repeat > 1 else 0

    def span(seq):
        return pl.ds(pl.multiple_of(seq * rows_dev, rows_dev), rows_dev)

    def wide_span(block):
        return pl.ds(pl.multiple_of(block * wide, wide), wide)

    def peer(step):
        turn = lax.rem(seq_me * repeat + source_me + step, parts)
        return (turn % repeat) * seq_count + turn // repeat

    def seq_peer(step):
        return lax.rem(seq_me + step, seq_count)

    block = held * seq_count
    first_filter = pl.multiple_of(source_me * block, block)
    loads = [
        pltpu.make_async_copy(
            filter_ref.at[pl.ds(first_filter, block)], filter_rows, load_sem.at[4]
        )
    ]
    for place, (source, target) in enumerate(
        (
            (output_gate_ref, output_gate),
            (input_gate_ref, input_gate),
            (signal_ref, signal),
            (cotangent_ref, cotangent),
        )
    ):
        loads.append(pltpu.make_async_copy(source, target, load_sem.at[place]))
    table_loads = [
        pltpu.make_async_copy(source, target, table_sem.at[place])
        for place, (source, target) in enumerate(zip(constants, tables_ref))
    ]
    for load in loads + table_loads:
        load.start()

    barrier = pltpu.get_barrier_semaphore()

    @pl.loop(1, parts)
    def _(step):
        pl.semaphore_signal(
            barrier, inc=1, device_id=device(peer(step)), device_id_type=pl.DeviceIdType.MESH
        )

    for load in loads:
        load.wait()

    @pl.loop(0, block // 8)
    def _(group):
        for row in range(rows_dev):
            taps_ref[pl.ds(group * (8 * rows_dev) + row, 8, stride=rows_dev)] = filter_rows[
                pl.ds(pl.multiple_of(group * 8, 8), 8), pl.ds(row * 128, 128)
            ]

    @pl.loop(0, channels // 16)
    def _(group):
        lines = pl.ds(pl.multiple_of(group * 16, 16), 16)
        for row in range(rows_dev):
            lanes = pl.ds(row * 128, 128)
            mixed = input_gate[lines, lanes].astype(jnp.float32) * signal[lines, lanes].astype(
                jnp.float32
            )
            gated = cotangent[lines, lanes].astype(jnp.float32) * output_gate[
                lines, lanes
            ].astype(jnp.float32)
            start = group * (16 * wide) + row
            send_ref[pl.ds(start, 16, stride=wide)] = mixed
            send_ref[pl.ds(start + rows_dev, 16, stride=wide)] = gated

    pl.semaphore_wait(barrier, parts - 1)

    def send_in(index):
        pltpu.make_async_copy(
            taps_ref.at[span(seq_me * held + index)], taps_all.at[index, span(seq_me)], taps_sem.at[index]
        ).start()

        @pl.loop(1, seq_count)
        def _(step):
            to = seq_peer(step)
            pltpu.make_async_remote_copy(
                src_ref=taps_ref.at[span(to * held + index)],
                dst_ref=taps_all.at[index, span(seq_me)],
                send_sem=taps_sent.at[index],
                recv_sem=taps_sem.at[index],
                device_id={"seq": to, "chan": chan_me},
                device_id_type=pl.DeviceIdType.MESH,
            ).start()

        pltpu.make_async_copy(
            send_ref.at[wide_span(place_me * held + index)],
            seqs.at[index, source_me, wide_span(seq_me)],
            in_sem.at[index],
        ).start()

        @pl.loop(1, parts)
        def _(step):
            to = peer(step)
            pltpu.make_async_remote_copy(
                src_ref=send_ref.at[wide_span(to * held + index)],
                dst_ref=seqs.at[index, source_me, wide_span(seq_me)],
                send_sem=in_sent.at[index],
                recv_sem=in_sem.at[index],
                device_id=device(to),
                device_id_type=pl.DeviceIdType.MESH,
            ).start()

    def send_out(index):
        mine = place_me * held + index
        pltpu.make_async_copy(
            kernels.at[index, span(seq_me)],
            kernel_ref.at[seq_me * held + index],
            kernel_sem,
        ).start()

        @pl.loop(1, seq_count)
        def _(step):
            to = seq_peer(step)
            pltpu.make_async_remote_copy(
                src_ref=kernels.at[index, span(to)],
                dst_ref=kernel_ref.at[seq_me * held + index],
                send_sem=kernel_sent.at[index],
                recv_sem=kernel_sem,
                device_id={"seq": to, "chan": chan_me},
                device_id_type=pl.DeviceIdType.MESH,
            ).start()

        pltpu.make_async_copy(
            outs.at[index, :, source_me, span(seq_me)], result_ref.at[:, mine], out_sem
        ).start()

        @pl.loop(1, parts)
        def _(step):
            to = peer(step)
            pltpu.make_async_remote_copy(
                src_ref=outs.at[index, :, chan_of(to), span(to % seq_count)],
                dst_ref=result_ref.at[:, mine],
                send_sem=out_sent.at[index],
                recv_sem=out_sem,
                device_id=device(to),
                device_id_type=pl.DeviceIdType.MESH,
            ).start()

    def finish(ref, sem):
        pltpu.make_async_copy(ref, ref, sem).wait()

    for index in range(held):
        send_in(index)

    for load in table_loads:
        load.wait()
    whole = [table[...] for table in tables_ref[:8]]
    tables_in = tuple(zip(whole[::2], whole[1::2])) + (tables_ref[8][0], tables_ref[8][1])

    def sequence(index, which, chan):
        lines = seqs[index, chan].reshape(seq_count, 2, rows_dev, 128)
        return lines[:, which].reshape(seq_count * rows_dev, 128)

    for index in range(held):
        finish(taps_all.at[index], taps_sem.at[index])
        finish(seqs.at[index], in_sem.at[index])
        mixed = [functools.partial(sequence, index, 0, c) for c in range(repeat)]
        gated = [functools.partial(sequence, index, 1, c) for c in range(repeat)]
        pairs, kernel = transform_channels(
            tables_in, mixed, gated, lambda: taps_all[index], scale
        )
        for chan, (response, grad) in enumerate(pairs):
            outs[index, 0, chan] = response
            outs[index, 1, chan] = grad
        kernels[index] = kernel
        send_out(index)

    for index in range(held):
        finish(send_ref.at[pl.ds(0, (parts - 1) * wide)], in_sent.at[index])
        finish(taps_ref.at[pl.ds(0, (seq_count - 1) * rows_dev)], taps_sent.at[index])
        finish(send_ref.at[pl.ds(0, (parts - 1) * wide)], out_sent.at[index])
        finish(taps_ref.at[pl.ds(0, (seq_count - 1) * rows_dev)], kernel_sent.at[index])
    finish(kernel_ref, kernel_sem)
    finish(result_ref, out_sem)


def exchange(inputs, repeat, seq_count, held):
    channels, tok_local = inputs[2].shape
    rows_dev = tok_local // 128
    rows = rows_dev * seq_count
    parts = repeat * seq_count
    constants = tables(rows, 128)
    hbm = pl.BlockSpec(memory_space=pl.ANY)
    f32 = jnp.float32
    dma = pltpu.SemaphoreType.DMA
    size = 2 * channels * tok_local
    return pl.pallas_call(
        functools.partial(
            exchange_kernel, repeat, seq_count, held, rows_dev, 1.0 / math.sqrt(rows * 128)
        ),
        in_specs=[hbm] * (5 + len(constants)),
        out_specs=[hbm, hbm],
        out_shape=[
            jax.ShapeDtypeStruct((2, channels, rows_dev, 128), f32),
            jax.ShapeDtypeStruct((seq_count * held, rows_dev, 128), f32),
        ],
        scratch_shapes=[pltpu.VMEM(table.shape, table.dtype) for table in constants]
        + [pltpu.VMEM((channels, tok_local), jnp.bfloat16)] * 4
        + [
            pltpu.VMEM((held * seq_count, tok_local), f32),
            pltpu.VMEM((channels * 2 * rows_dev, 128), f32),
            pltpu.VMEM((held * seq_count * rows_dev, 128), f32),
            pltpu.VMEM((held, repeat, 2 * rows, 128), f32),
            pltpu.VMEM((held, rows, 128), f32),
            pltpu.VMEM((held, 2, repeat, rows, 128), f32),
            pltpu.VMEM((held, rows, 128), f32),
            dma((5,)), dma((len(constants),)),
            dma((held,)), dma((held,)), dma(()), dma(()),
            dma((held,)), dma((held,)), dma((held,)), dma((held,)),
        ],
        compiler_params=pltpu.CompilerParams(
            collective_id=0, has_side_effects=True, vmem_limit_bytes=64 * 1024 * 1024
        ),
        cost_estimate=pl.CostEstimate(
            flops=48 * size * (rows + 128), bytes_accessed=8 * size, transcendentals=0
        ),
        name="exchange",
    )(*inputs, *constants)


def per_device(output_gate, input_gate, signal, cotangent, long_filter):
    seq_count = lax.axis_size("seq")
    chan_count = lax.axis_size("chan")
    channels, tok_local = signal.shape
    filters = long_filter.shape[0]
    spread = channels == filters and filters % (seq_count * chan_count) == 0
    repeat = chan_count if spread else 1
    held = filters // (seq_count * repeat)

    results, kernel = exchange(
        (output_gate, input_gate, signal, cotangent, long_filter), repeat, seq_count, held
    )

    kernel = kernel.reshape(held * seq_count, tok_local)
    if not spread:
        kernel = lax.psum_scatter(kernel, "chan", scatter_dimension=0, tiled=True)
    response, grad_mixed = results.reshape(2, channels, tok_local)
    grad_output_gate = (cotangent.astype(jnp.float32) * response).astype(jnp.bfloat16)
    grad_input_gate = (grad_mixed * signal.astype(jnp.float32)).astype(jnp.bfloat16)
    grad_signal = (grad_mixed * input_gate.astype(jnp.float32)).astype(jnp.bfloat16)
    return (grad_output_gate, grad_input_gate, grad_signal, kernel)


def solution(mesh):
    placed = (
        P("chan", "seq"),
        P("chan", "seq"),
        P("chan", "seq"),
        P("chan", "seq"),
        P(None, "seq"),
    )
    return jax.shard_map(
        per_device,
        mesh=mesh,
        in_specs=placed,
        out_specs=(P("chan", "seq"), P("chan", "seq"), P("chan", "seq"), P("chan", "seq")),
        check_vma=False,
    )
```
